256 devices in a mesh: row: 16 (over z_lo, x, core), col: 16 (over y, z_hi).
Axes of the slice: x: 4, y: 4, z: 8 (z_hi: 4, z_lo: 2; z = z_hi * 2 + z_lo), core: 2. Of those that a mesh axis runs over, the one named last changes fastest.
Arguments:
- examples: bfloat16 [262144, 512], P(('row', 'col')), may hold values from -2700 to 2700
- queries: bfloat16 [4096, 512], P('col'), may hold values from -0.25 to 0.25
Outputs:
- whitened: float32 [262144, 512], P(('row', 'col'))
- scores: float32 [262144], P(('row', 'col'))
The draws below stay inside these ranges and needn't reach their ends.
All inputs are finite; a program needn't handle non-finite values.
Results may differ from the reference program's by a relative error of at most 0.00086.
Values may be sent and summed in bfloat16 or wider, within the bound.
No kernel may reach another device: no remote copies, remote signals or barrier semaphores. Data moves between devices by JAX's collectives and lax.ppermute only.
A program may use at most 64 MiB of HBM per device.

```python
import math
import jax
import jax.numpy as jnp
from jax import lax

K = 512
ROWS_DEV = 1024
EXAMPLES = 262144
QUERIES = 4096


def draw_examples(key, part):
    key = jax.random.fold_in(key, 11)
    first, second, third = jax.random.split(key, 3)
    rows = jnp.arange(EXAMPLES)
    block = (rows // ROWS_DEV).astype(jnp.float32)
    last = max(EXAMPLES // ROWS_DEV - 1, 1)
    row_scale = jnp.exp(jax.random.uniform(second, (EXAMPLES, 1), jnp.float32) * math.log(10.0))
    col_scale = jnp.exp(jax.random.uniform(third, (1, K), jnp.float32) * math.log(10.0))
    base = jnp.clip(jax.random.normal(first, (EXAMPLES, K), jnp.float32), -5.0, 5.0)
    ramp = jnp.exp(block / last * math.log(4.0))
    return (base * row_scale * ramp[:, None] * col_scale).astype(jnp.bfloat16)


def shard_levels(key, shape, cuts, least, top_value):
    factor_of, own = 1.0, jax.random.fold_in(key, 6)
    for axis_at, shards_of in cuts:
        steps = jnp.exp(jax.random.uniform(jax.random.fold_in(own, axis_at), (shards_of,), jnp.float32, least / len(cuts), top_value / len(cuts)))
        factor_of = factor_of * jnp.repeat(steps, shape[axis_at] // shards_of).reshape([-1 if axis == axis_at else 1 for axis in range(len(shape))])
    return factor_of


def centred(rng, extent, deviation, reach, shards=(), kind=jnp.bfloat16):
    gain = shard_levels(rng, extent, shards, -0.22, 0.18) if shards else 1.0
    entries = jax.random.normal(rng, extent, jnp.float32) * deviation * gain
    return jnp.minimum(jnp.maximum(entries, -reach), reach).astype(kind)


def setup_inputs(seed: int = 0) -> dict:
    keys = jax.random.split(jax.random.key(seed), 3)
    examples = draw_examples(jax.random.fold_in(keys[2], 71), 0)
    queries = centred(keys[1], (QUERIES, K), K ** -0.5, 0.25, ((0, 16),))
    return {"examples": examples, "queries": queries}


def reference(examples, queries):
    gram = lax.dot_general(examples.astype(jnp.float32), examples.astype(jnp.float32), (((0,), (0,)), ((), ())), preferred_element_type=jnp.float32)
    lower = jnp.linalg.cholesky(gram)
    identity = jnp.eye(K, dtype=jnp.float32)
    inverse = lax.linalg.triangular_solve(lower, identity, left_side=True, lower=True, transpose_a=True)
    factor = jnp.sqrt(jnp.float32(EXAMPLES))
    whitened = factor * jnp.dot(examples.astype(jnp.float32), inverse, precision=lax.Precision.HIGHEST)
    rounded = whitened.astype(jnp.bfloat16)
    blocks = rounded.reshape(EXAMPLES // ROWS_DEV, ROWS_DEV, K)
    panel = queries.astype(jnp.float32)

    def best_block(block):
        values = lax.dot_general(block.astype(jnp.float32), panel, (((1,), (1,)), ((), ())), precision=lax.Precision.HIGHEST)
        return lax.optimization_barrier(jnp.max(values, axis=1))
    scores = lax.map(best_block, blocks).reshape(EXAMPLES)
    return (whitened, scores)
```

```python
import functools

import jax
import jax.numpy as jnp
from jax import lax
from jax.experimental import pallas as pl
from jax.experimental.pallas import tpu as pltpu
from jax.sharding import Mesh, PartitionSpec as P

FINE = ("z_lo", "x", "core", "y", "z_hi")
B = 128
W = 8
VMEM = pl.BlockSpec(memory_space=pltpu.VMEM)
SMEM = pl.BlockSpec(memory_space=pltpu.SMEM)


def exact_dot(a, b, dims):
    return lax.dot_general(
        a, b, (dims, ((), ())), precision=lax.Precision.HIGHEST, preferred_element_type=jnp.float32
    )


def gram_kernel(core_ref, x_ref, mine_ref, other_ref, packed):
    width = x_ref.shape[1]
    count = width // B
    at = 0
    for i in range(0, count, 2):
        left = x_ref[:, i * B : (i + 2) * B]
        part = lax.dot_general(
            left, x_ref[:, i * B :], (((0,), (0,)), ((), ())), preferred_element_type=jnp.float32
        )
        for r in range(2):
            for j in range(i + r, count):
                packed[at * B : (at + 1) * B, :] = part[r * B : (r + 1) * B, (j - i) * B : (j - i + 1) * B]
                at += 1
    half = mine_ref.shape[0]
    core = core_ref[0]
    mine_ref[...] = packed[pl.ds(pl.multiple_of(core * half, 8), half), :]
    other_ref[...] = packed[pl.ds(pl.multiple_of((1 - core) * half, 8), half), :]


def local_gram(core, x):
    count = x.shape[1] // B
    rows = count * (count + 1) // 2 * B
    half = jax.ShapeDtypeStruct((rows // 2, B), jnp.float32)
    return pl.pallas_call(
        gram_kernel,
        out_shape=(half, half),
        in_specs=[SMEM, VMEM],
        out_specs=(VMEM, VMEM),
        scratch_shapes=[pltpu.VMEM((rows, B), jnp.float32)],
        compiler_params=pltpu.CompilerParams(vmem_limit_bytes=32 << 20),
        name="gram",
    )(core, x)


def eliminate(a):
    n = a.shape[0]
    lane = lax.broadcasted_iota(jnp.int32, (W, n), 1)
    sub = lax.broadcasted_iota(jnp.int32, (W, n), 0)
    out = []
    for p in range(n // W):
        top, rest = a[:W], a[W:]
        c = p * W
        here = (lane >= c) & (lane < c + W)
        cols = [jnp.broadcast_to(top[:, c + k : c + k + 1], (W, n)) for k in range(W)]
        low = jnp.where(here, jnp.where(lane - c == sub, 1.0, 0.0), top)
        full = low
        pivots = jnp.ones((W, n), jnp.float32)
        for j in range(W):
            pivot = jnp.broadcast_to(cols[j][j : j + 1], (W, n))
            ratio = jnp.where(sub == j, 0.0, cols[j] * (1.0 / pivot))
            pivots = jnp.where(sub == j, pivot, pivots)
            for k in range(j + 1, W):
                cols[k] = cols[k] - ratio * jnp.broadcast_to(cols[k][j : j + 1], (W, n))
            full = full - ratio * jnp.broadcast_to(full[j : j + 1], (W, n))
            low = low - jnp.where(sub > j, ratio, 0.0) * jnp.broadcast_to(low[j : j + 1], (W, n))
        out.append(jnp.where(lane < c + W, low * lax.rsqrt(pivots), 0.0))
        if p < n // W - 1:
            full = full * (1.0 / pivots)
            h = rest.shape[0]
            wide = lax.broadcasted_iota(jnp.int32, (h, n), 1)
            a = jnp.where((wide >= c) & (wide < c + W), 0.0, rest)
            for k in range(W):
                a = a - jnp.broadcast_to(rest[:, c + k : c + k + 1], (h, n)) * jnp.broadcast_to(
                    full[k : k + 1], (h, n)
                )
    return jnp.concatenate(out, 0)


def factor_kernel(core_ref, mine_ref, other_ref, o_ref, packed, s_ref):
    half = mine_ref.shape[0]
    core = core_ref[0]
    packed[pl.ds(pl.multiple_of(core * half, 8), half), :] = mine_ref[...]
    packed[pl.ds(pl.multiple_of((1 - core) * half, 8), half), :] = other_ref[...]
    n = o_ref.shape[0]
    count = n // B
    at = 0
    for i in range(count):
        for j in range(i, count):
            s_ref[i * B : (i + 1) * B, j * B : (j + 1) * B] = packed[at * B : (at + 1) * B, :]
            at += 1
    for k in range(count):
        r = slice(k * B, (k + 1) * B)
        inv = eliminate(s_ref[r, r])
        o_ref[r, r] = inv
        if k > 0:
            o_ref[r, : k * B] = exact_dot(inv, s_ref[r, : k * B], ((1,), (0,)))
        if k < count - 1:
            right = exact_dot(inv, s_ref[r, (k + 1) * B :], ((1,), (0,)))
            o_ref[r, (k + 1) * B :] = jnp.zeros((B, n - (k + 1) * B), jnp.float32)
            left = o_ref[r, : (k + 1) * B]
            for i in range(k + 1, count):
                ri = slice(i * B, (i + 1) * B)
                coef = right[:, (i - k - 1) * B : (i - k) * B]
                s_ref[ri, i * B :] = s_ref[ri, i * B :] - exact_dot(coef, right[:, (i - k - 1) * B :], ((0,), (0,)))
                new = exact_dot(coef, left, ((0,), (0,)))
                if k > 0:
                    s_ref[ri, : k * B] = s_ref[ri, : k * B] - new[:, : k * B]
                s_ref[ri, r] = -new[:, k * B :]


def inverse_factor(core, mine, other, n):
    return pl.pallas_call(
        factor_kernel,
        out_shape=jax.ShapeDtypeStruct((n, n), jnp.float32),
        in_specs=[SMEM, VMEM, VMEM],
        out_specs=VMEM,
        scratch_shapes=[pltpu.VMEM((2 * mine.shape[0], B), jnp.float32), pltpu.VMEM((n, n), jnp.float32)],
        compiler_params=pltpu.CompilerParams(vmem_limit_bytes=32 << 20),
        name="factor",
    )(core, mine, other)


def sum_gram(mine, other):
    swap = [(0, 1), (1, 0)]
    plane = lax.axis_size("x") * lax.axis_size("y")
    depth = lax.axis_size("z_lo") * lax.axis_size("z_hi")
    mine = mine + lax.ppermute(other, "core", swap)
    parts = lax.all_to_all(mine.reshape(plane, -1, B), ("x", "y"), 0, 0)
    part = jnp.sum(parts, 0)
    parts = lax.all_to_all(jnp.broadcast_to(part[None], (depth, *part.shape)), ("z_lo", "z_hi"), 0, 0)
    part = jnp.sum(parts, 0)
    parts = lax.all_to_all(jnp.broadcast_to(part[None], (plane, *part.shape)), ("x", "y"), 0, 0)
    mine = parts.reshape(mine.shape)
    return mine, lax.ppermute(mine, "core", swap)


def score_kernel(scale, x_ref, inv_ref, q_ref, w_ref, s_ref):
    inv = inv_ref[...]
    high = inv.astype(jnp.bfloat16)
    low = (inv - high.astype(jnp.float32)).astype(jnp.bfloat16)
    x = x_ref[...]
    dims = (((1,), (1,)), ((), ()))
    whitened = scale * (
        lax.dot_general(x, high, dims, preferred_element_type=jnp.float32)
        + lax.dot_general(x, low, dims, preferred_element_type=jnp.float32)
    )
    w_ref[...] = whitened
    rounded = whitened.astype(jnp.bfloat16)
    step = 512
    best = None
    for m in range(0, q_ref.shape[0], step):
        values = lax.dot_general(rounded, q_ref[m : m + step, :], dims, preferred_element_type=jnp.float32)
        for t in range(0, step, B):
            part = values[:, t : t + B]
            best = part if best is None else jnp.maximum(best, part)
    s_ref[...] = jnp.max(best, axis=1, keepdims=True)


def whiten_and_score(x, inv, queries, scale):
    rows, width = x.shape
    tile = 256
    return pl.pallas_call(
        functools.partial(score_kernel, scale),
        grid=(rows // tile,),
        out_shape=(
            jax.ShapeDtypeStruct((rows, width), jnp.float32),
            jax.ShapeDtypeStruct((rows, 1), jnp.float32),
        ),
        in_specs=[
            pl.BlockSpec((tile, width), lambda i: (i, 0)),
            VMEM,
            VMEM,
        ],
        out_specs=(
            pl.BlockSpec((tile, width), lambda i: (i, 0)),
            pl.BlockSpec((tile, 1), lambda i: (i, 0)),
        ),
        compiler_params=pltpu.CompilerParams(vmem_limit_bytes=48 << 20),
        name="score",
    )(x, inv, queries)


def body(examples, queries):
    rows, width = examples.shape
    core = lax.axis_index("core").astype(jnp.int32).reshape(1)
    queries = lax.all_gather(queries, ("y", "z_hi"), axis=0, tiled=True)
    mine, other = local_gram(core, examples)
    mine, other = sum_gram(mine, other)
    inv = inverse_factor(core, mine, other, width)
    count = rows
    for axis in FINE:
        count *= lax.axis_size(axis)
    whitened, scores = whiten_and_score(examples, inv, queries, float(count) ** 0.5)
    return whitened, scores.reshape(rows)


def solution(mesh):
    fine = Mesh(mesh.devices.reshape(2, 4, 2, 4, 4), FINE)
    placed = (P(FINE, None), P(("y", "z_hi"), None))
    return jax.shard_map(
        body, mesh=fine, in_specs=placed, out_specs=(P(FINE, None), P(FINE)), check_vma=False
    )
```

```python
import functools

import jax
import jax.numpy as jnp
from jax import lax
from jax.experimental import pallas as pl
from jax.experimental.pallas import tpu as pltpu
from jax.sharding import Mesh, PartitionSpec as P

FINE = ("z_lo", "x", "core", "y", "z_hi")
B = 128
SWAP = [(0, 1), (1, 0)]
W = 8
VMEM = pl.BlockSpec(memory_space=pltpu.VMEM)
SMEM = pl.BlockSpec(memory_space=pltpu.SMEM)


def exact_dot(a, b, dims):
    return lax.dot_general(
        a, b, (dims, ((), ())), precision=lax.Precision.HIGHEST, preferred_element_type=jnp.float32
    )


def gram_kernel(core_ref, x_ref, mine_ref, other_ref, packed):
    width = x_ref.shape[1]
    count = width // B
    at = 0
    for i in range(0, count, 2):
        left = x_ref[:, i * B : (i + 2) * B]
        part = lax.dot_general(
            left, x_ref[:, i * B :], (((0,), (0,)), ((), ())), preferred_element_type=jnp.float32
        )
        for r in range(2):
            for j in range(i + r, count):
                packed[at * B : (at + 1) * B, :] = part[r * B : (r + 1) * B, (j - i) * B : (j - i + 1) * B]
                at += 1
    half = mine_ref.shape[0]
    core = core_ref[0]
    mine_ref[...] = packed[pl.ds(pl.multiple_of(core * half, 8), half), :]
    other_ref[...] = packed[pl.ds(pl.multiple_of((1 - core) * half, 8), half), :]


def local_gram(core, x):
    count = x.shape[1] // B
    rows = count * (count + 1) // 2 * B
    half = jax.ShapeDtypeStruct((rows // 2, B), jnp.float32)
    return pl.pallas_call(
        gram_kernel,
        out_shape=(half, half),
        in_specs=[SMEM, VMEM],
        out_specs=(VMEM, VMEM),
        scratch_shapes=[pltpu.VMEM((rows, B), jnp.float32)],
        compiler_params=pltpu.CompilerParams(vmem_limit_bytes=32 << 20),
        name="gram",
    )(core, x)


def eliminate(a):
    n = a.shape[0]
    lane = lax.broadcasted_iota(jnp.int32, (W, n), 1)
    sub = lax.broadcasted_iota(jnp.int32, (W, n), 0)
    out = []
    for p in range(n // W):
        top, rest = a[:W], a[W:]
        c = p * W
        here = (lane >= c) & (lane < c + W)
        cols = [jnp.broadcast_to(top[:, c + k : c + k + 1], (W, n)) for k in range(W)]
        low = jnp.where(here, jnp.where(lane - c == sub, 1.0, 0.0), top)
        full = low
        pivots = jnp.ones((W, n), jnp.float32)
        for j in range(W):
            pivot = jnp.broadcast_to(cols[j][j : j + 1], (W, n))
            ratio = jnp.where(sub == j, 0.0, cols[j] * (1.0 / pivot))
            pivots = jnp.where(sub == j, pivot, pivots)
            for k in range(j + 1, W):
                cols[k] = cols[k] - ratio * jnp.broadcast_to(cols[k][j : j + 1], (W, n))
            full = full - ratio * jnp.broadcast_to(full[j : j + 1], (W, n))
            low = low - jnp.where(sub > j, ratio, 0.0) * jnp.broadcast_to(low[j : j + 1], (W, n))
        out.append(jnp.where(lane < c + W, low * lax.rsqrt(pivots), 0.0))
        if p < n // W - 1:
            full = full * (1.0 / pivots)
            h = rest.shape[0]
            wide = lax.broadcasted_iota(jnp.int32, (h, n), 1)
            a = jnp.where((wide >= c) & (wide < c + W), 0.0, rest)
            for k in range(W):
                a = a - jnp.broadcast_to(rest[:, c + k : c + k + 1], (h, n)) * jnp.broadcast_to(
                    full[k : k + 1], (h, n)
                )
    return jnp.concatenate(out, 0)


def factor_kernel(core_ref, mine_ref, other_ref, o_ref, packed, s_ref):
    half = mine_ref.shape[0]
    core = core_ref[0]
    packed[pl.ds(pl.multiple_of(core * half, 8), half), :] = mine_ref[...]
    packed[pl.ds(pl.multiple_of((1 - core) * half, 8), half), :] = other_ref[...]
    n = o_ref.shape[0]
    count = n // B
    at = 0
    for i in range(count):
        for j in range(i, count):
            s_ref[i * B : (i + 1) * B, j * B : (j + 1) * B] = packed[at * B : (at + 1) * B, :]
            at += 1
    for k in range(count):
        r = slice(k * B, (k + 1) * B)
        inv = eliminate(s_ref[r, r])
        o_ref[r, r] = inv
        if k > 0:
            o_ref[r, : k * B] = exact_dot(inv, s_ref[r, : k * B], ((1,), (0,)))
        if k < count - 1:
            right = exact_dot(inv, s_ref[r, (k + 1) * B :], ((1,), (0,)))
            o_ref[r, (k + 1) * B :] = jnp.zeros((B, n - (k + 1) * B), jnp.float32)
            left = o_ref[r, : (k + 1) * B]
            for i in range(k + 1, count):
                ri = slice(i * B, (i + 1) * B)
                coef = right[:, (i - k - 1) * B : (i - k) * B]
                s_ref[ri, i * B :] = s_ref[ri, i * B :] - exact_dot(coef, right[:, (i - k - 1) * B :], ((0,), (0,)))
                new = exact_dot(coef, left, ((0,), (0,)))
                if k > 0:
                    s_ref[ri, : k * B] = s_ref[ri, : k * B] - new[:, : k * B]
                s_ref[ri, r] = -new[:, k * B :]


def inverse_factor(core, mine, other, n):
    return pl.pallas_call(
        factor_kernel,
        out_shape=jax.ShapeDtypeStruct((n, n), jnp.float32),
        in_specs=[SMEM, VMEM, VMEM],
        out_specs=VMEM,
        scratch_shapes=[pltpu.VMEM((2 * mine.shape[0], B), jnp.float32), pltpu.VMEM((n, n), jnp.float32)],
        compiler_params=pltpu.CompilerParams(vmem_limit_bytes=32 << 20),
        name="factor",
    )(core, mine, other)


def ring(axis):
    n = lax.axis_size(axis)
    return [[(i, (i - k) % n) for i in range(n)] for k in range(1, n)]


def gather(own, axis):
    return [own] + [lax.ppermute(own, axis, step) for step in ring(axis)]


def body(examples, queries):
    rows, width = examples.shape
    plane = lax.axis_size("x") * lax.axis_size("y")
    depth = lax.axis_size("z_lo") * lax.axis_size("z_hi")
    index = lax.axis_index("core").astype(jnp.int32)
    share = queries.shape[0] // (2 * lax.axis_size("x"))
    start = (index * lax.axis_size("x") + lax.axis_index("x")) * share
    piece = lax.dynamic_slice_in_dim(queries, start, share, 0)
    pieces = gather(piece, "z_hi")

    core = index.reshape(1)
    mine, other = local_gram(core, examples)
    mine = mine + lax.ppermute(other, "core", SWAP)
    part = jnp.sum(lax.all_to_all(mine.reshape(plane, -1, B), ("x", "y"), 0, 0), 0)

    pieces, part = lax.optimization_barrier((pieces, part))
    pieces = gather(jnp.concatenate(pieces, 0), "y")

    spread = jnp.broadcast_to(part[None], (depth, *part.shape))
    part = jnp.sum(lax.all_to_all(spread, ("z_lo", "z_hi"), 0, 0), 0)

    pieces, part = lax.optimization_barrier((pieces, part))
    pieces = gather(jnp.concatenate(pieces, 0), "x")

    spread = jnp.broadcast_to(part[None], (plane, *part.shape))
    mine = lax.all_to_all(spread, ("x", "y"), 0, 0).reshape(mine.shape)
    other = lax.ppermute(mine, "core", SWAP)
    inv = inverse_factor(core, mine, other, width)

    pieces, inv = lax.optimization_barrier((pieces, inv))
    pieces = pieces + [lax.ppermute(p, "core", SWAP) for p in pieces]
    count = rows
    for axis in FINE:
        count *= lax.axis_size(axis)
    return whiten_and_score(examples, inv, pieces, float(count) ** 0.5)


def score_kernel(scale, step, x_ref, inv_ref, *refs):
    *q_refs, w_ref, s_ref, high, low = refs
    n = inv_ref.shape[0]

    @pl.when(pl.program_id(0) == 0)
    def _():
        inv = inv_ref[...] * scale
        high[...] = inv.astype(jnp.bfloat16)
        low[...] = (inv - high[...].astype(jnp.float32)).astype(jnp.bfloat16)

    dims = (((1,), (1,)), ((), ()))
    x = x_ref[...]
    rounded = []
    wide = 2 * B
    for at in range(0, n, wide):
        end = at + wide
        part = lax.dot_general(
            x[:, :end], high[at:end, :end], dims, preferred_element_type=jnp.float32
        ) + lax.dot_general(x[:, :end], low[at:end, :end], dims, preferred_element_type=jnp.float32)
        w_ref[:, at:end] = part
        rounded.append(part.astype(jnp.bfloat16))
    rounded = jnp.concatenate(rounded, 1)
    best = None
    for q_ref in q_refs:
        for m in range(0, q_ref.shape[0], step):
            values = lax.dot_general(
                q_ref[m : m + step, :], rounded, dims, preferred_element_type=jnp.float32
            )
            values = jnp.max(values.reshape(step // 8, 8, values.shape[1]), axis=0)
            best = values if best is None else jnp.maximum(best, values)
    s_ref[...] = jnp.max(best, axis=0, keepdims=True)


def whiten_and_score(x, inv, queries, scale):
    rows, width = x.shape
    tile = 512
    whitened, scores = pl.pallas_call(
        functools.partial(score_kernel, scale, 512),
        grid=(rows // tile,),
        out_shape=(
            jax.ShapeDtypeStruct((rows, width), jnp.float32),
            jax.ShapeDtypeStruct((1, rows), jnp.float32),
        ),
        in_specs=[pl.BlockSpec((tile, width), lambda i: (i, 0)), VMEM] + [VMEM] * len(queries),
        out_specs=(
            pl.BlockSpec((tile, width), lambda i: (i, 0)),
            pl.BlockSpec((1, tile), lambda i: (0, i)),
        ),
        scratch_shapes=[pltpu.VMEM((width, width), jnp.bfloat16)] * 2,
        compiler_params=pltpu.CompilerParams(vmem_limit_bytes=48 << 20),
        name="score",
    )(x, inv, *queries)
    return whitened, scores.reshape(rows)


def solution(mesh):
    fine = Mesh(mesh.devices.reshape(2, 4, 2, 4, 4), FINE)
    placed = (P(FINE, None), P(("y", "z_hi"), None))
    return jax.shard_map(
        body, mesh=fine, in_specs=placed, out_specs=(P(FINE, None), P(FINE)), check_vma=False
    )
```

```python
import functools

import jax
import jax.numpy as jnp
from jax import lax
from jax.experimental import pallas as pl
from jax.experimental.pallas import tpu as pltpu
from jax.sharding import Mesh, PartitionSpec as P

FINE = ("z_lo", "x", "core", "y", "z_hi")
B = 128
SWAP = [(0, 1), (1, 0)]
W = 16
VMEM = pl.BlockSpec(memory_space=pltpu.VMEM)
SMEM = pl.BlockSpec(memory_space=pltpu.SMEM)


def exact_dot(a, b, dims):
    return lax.dot_general(
        a, b, (dims, ((), ())), precision=lax.Precision.HIGHEST, preferred_element_type=jnp.float32
    )


def gram_kernel(core_ref, x_ref, mine_ref, other_ref, packed):
    width = x_ref.shape[1]
    count = width // B
    at = 0
    for i in range(0, count, 2):
        left = x_ref[:, i * B : (i + 2) * B]
        part = lax.dot_general(
            left, x_ref[:, i * B :], (((0,), (0,)), ((), ())), preferred_element_type=jnp.float32
        )
        for r in range(2):
            for j in range(i + r, count):
                packed[at * B : (at + 1) * B, :] = part[r * B : (r + 1) * B, (j - i) * B : (j - i + 1) * B]
                at += 1
    half = mine_ref.shape[0]
    core = core_ref[0]
    mine_ref[...] = packed[pl.ds(pl.multiple_of(core * half, 8), half), :]
    other_ref[...] = packed[pl.ds(pl.multiple_of((1 - core) * half, 8), half), :]


def local_gram(core, x):
    count = x.shape[1] // B
    rows = count * (count + 1) // 2 * B
    half = jax.ShapeDtypeStruct((rows // 2, B), jnp.float32)
    return pl.pallas_call(
        gram_kernel,
        out_shape=(half, half),
        in_specs=[SMEM, VMEM],
        out_specs=(VMEM, VMEM),
        scratch_shapes=[pltpu.VMEM((rows, B), jnp.float32)],
        compiler_params=pltpu.CompilerParams(vmem_limit_bytes=32 << 20),
        name="gram",
    )(core, x)


def spread(x, lane):
    return jnp.take_along_axis(x, jnp.full(x.shape, lane, jnp.int32), axis=1)


def tree_sum(terms):
    terms = list(terms)
    while len(terms) > 1:
        pairs = [a + b for a, b in zip(terms[::2], terms[1::2])]
        terms = pairs + terms[len(pairs) * 2 :]
    return terms[0]


def gram_of_rows(s):
    high = s.astype(jnp.bfloat16)
    rest = s - high.astype(jnp.float32)
    mid = rest.astype(jnp.bfloat16)
    low = (rest - mid.astype(jnp.float32)).astype(jnp.bfloat16)
    return lax.dot_general(
        jnp.concatenate([high, high, mid, high, low, mid], 0),
        jnp.concatenate([high, mid, high, low, high, mid], 0),
        (((0,), (0,)), ((), ())),
        preferred_element_type=jnp.float32,
    )


def eliminate(a):
    n = a.shape[0]
    panels = n // W
    lane = lax.broadcasted_iota(jnp.int32, (W, n), 1)
    sub = lax.broadcasted_iota(jnp.int32, (W, n), 0)

    def row(x, j):
        return jnp.broadcast_to(x[j : j + 1], (W, n))

    out = []
    groups = [a[p * W : (p + 1) * W] for p in range(panels)]
    for p in range(panels):
        c = p * W
        here = (lane >= c) & (lane < c + W)
        cols = [spread(groups[p], c + k) for k in range(W)]
        low = jnp.where(here, jnp.where(lane - c == sub, 1.0, 0.0), groups[p])
        full = low
        inverse = jnp.ones((W, n), jnp.float32)
        for j in range(W):
            one = 1.0 / row(cols[j], j)
            ratio = jnp.where(sub == j, 0.0, cols[j] * one)
            inverse = jnp.where(sub == j, one, inverse)
            for k in range(j + 1, W):
                cols[k] = cols[k] - ratio * row(cols[k], j)
            full = full - ratio * row(full, j)
            low = low - jnp.where(sub > j, ratio, 0.0) * row(low, j)
        low = low * (lax.rsqrt(inverse) * inverse)
        out.append(jnp.where(lane < c + W, low, 0.0))
        if p < panels - 1:
            full = full * inverse
            near = tree_sum(spread(groups[p + 1], c + k) * row(full, k) for k in range(W))
            groups[p + 1] = jnp.where(here, 0.0, groups[p + 1]) - near
            if p < panels - 2:
                far = gram_of_rows(low)
                for g in range(p + 2, panels):
                    groups[g] = jnp.where(here, 0.0, groups[g]) - far[g * W : (g + 1) * W]
    return jnp.concatenate(out, 0)


def factor_kernel(core_ref, mine_ref, other_ref, o_ref, packed, s_ref):
    half = mine_ref.shape[0]
    core = core_ref[0]
    packed[pl.ds(pl.multiple_of(core * half, 8), half), :] = mine_ref[...]
    packed[pl.ds(pl.multiple_of((1 - core) * half, 8), half), :] = other_ref[...]
    n = o_ref.shape[0]
    count = n // B
    at = 0
    for i in range(count):
        for j in range(i, count):
            s_ref[i * B : (i + 1) * B, j * B : (j + 1) * B] = packed[at * B : (at + 1) * B, :]
            at += 1
    for k in range(count):
        r = slice(k * B, (k + 1) * B)
        inv = eliminate(s_ref[r, r])
        o_ref[r, r] = inv
        if k > 0:
            o_ref[r, : k * B] = exact_dot(inv, s_ref[r, : k * B], ((1,), (0,)))
        if k < count - 1:
            right = exact_dot(inv, s_ref[r, (k + 1) * B :], ((1,), (0,)))
            o_ref[r, (k + 1) * B :] = jnp.zeros((B, n - (k + 1) * B), jnp.float32)
            left = o_ref[r, : (k + 1) * B]
            for i in range(k + 1, count):
                ri = slice(i * B, (i + 1) * B)
                coef = right[:, (i - k - 1) * B : (i - k) * B]
                s_ref[ri, i * B :] = s_ref[ri, i * B :] - exact_dot(coef, right[:, (i - k - 1) * B :], ((0,), (0,)))
                new = exact_dot(coef, left, ((0,), (0,)))
                if k > 0:
                    s_ref[ri, : k * B] = s_ref[ri, : k * B] - new[:, : k * B]
                s_ref[ri, r] = -new[:, k * B :]


def inverse_factor(core, mine, other, n):
    return pl.pallas_call(
        factor_kernel,
        out_shape=jax.ShapeDtypeStruct((n, n), jnp.float32),
        in_specs=[SMEM, VMEM, VMEM],
        out_specs=VMEM,
        scratch_shapes=[pltpu.VMEM((2 * mine.shape[0], B), jnp.float32), pltpu.VMEM((n, n), jnp.float32)],
        compiler_params=pltpu.CompilerParams(vmem_limit_bytes=32 << 20),
        name="factor",
    )(core, mine, other)


def ring(axis):
    n = lax.axis_size(axis)
    return [[(i, (i - k) % n) for i in range(n)] for k in range(1, n)]


def gather(own, axis):
    return [own] + [lax.ppermute(own, axis, step) for step in ring(axis)]


def body(examples, queries):
    rows, width = examples.shape
    plane = lax.axis_size("x") * lax.axis_size("y")
    depth = lax.axis_size("z_lo") * lax.axis_size("z_hi")
    index = lax.axis_index("core").astype(jnp.int32)
    share = queries.shape[0] // (2 * lax.axis_size("x"))
    start = (index * lax.axis_size("x") + lax.axis_index("x")) * share
    piece = lax.dynamic_slice_in_dim(queries, start, share, 0)
    pieces = gather(piece, "z_hi")

    core = index.reshape(1)
    mine, other = local_gram(core, examples)
    mine = mine + lax.ppermute(other, "core", SWAP)
    part = jnp.sum(lax.all_to_all(mine.reshape(plane, -1, B), ("x", "y"), 0, 0), 0)

    pieces, part = lax.optimization_barrier((pieces, part))
    pieces = gather(jnp.concatenate(pieces, 0), "y")

    spread = jnp.broadcast_to(part[None], (depth, *part.shape))
    part = jnp.sum(lax.all_to_all(spread, ("z_lo", "z_hi"), 0, 0), 0)

    pieces, part = lax.optimization_barrier((pieces, part))
    pieces = gather(jnp.concatenate(pieces, 0), "x")

    spread = jnp.broadcast_to(part[None], (plane, *part.shape))
    mine = lax.all_to_all(spread, ("x", "y"), 0, 0).reshape(mine.shape)
    other = lax.ppermute(mine, "core", SWAP)
    inv = inverse_factor(core, mine, other, width)

    pieces, inv = lax.optimization_barrier((pieces, inv))
    pieces = pieces + [lax.ppermute(p, "core", SWAP) for p in pieces]
    count = rows
    for axis in FINE:
        count *= lax.axis_size(axis)
    return whiten_and_score(examples, inv, pieces, float(count) ** 0.5)


def score_kernel(scale, step, x_ref, inv_ref, *refs):
    *q_refs, w_ref, s_ref, high, low = refs
    n = inv_ref.shape[0]

    @pl.when(pl.program_id(0) == 0)
    def _():
        inv = inv_ref[...] * scale
        high[...] = inv.astype(jnp.bfloat16)
        low[...] = (inv - high[...].astype(jnp.float32)).astype(jnp.bfloat16)

    dims = (((1,), (1,)), ((), ()))
    x = x_ref[...]
    rounded = []
    wide = 2 * B
    for at in range(0, n, wide):
        end = at + wide
        part = lax.dot_general(
            x[:, :end], high[at:end, :end], dims, preferred_element_type=jnp.float32
        ) + lax.dot_general(x[:, :end], low[at:end, :end], dims, preferred_element_type=jnp.float32)
        w_ref[:, at:end] = part
        rounded.append(part.astype(jnp.bfloat16))
    rounded = jnp.concatenate(rounded, 1)
    best = None
    for q_ref in q_refs:
        for m in range(0, q_ref.shape[0], step):
            values = lax.dot_general(
                q_ref[m : m + step, :], rounded, dims, preferred_element_type=jnp.float32
            )
            values = jnp.max(values.reshape(step // 8, 8, values.shape[1]), axis=0)
            best = values if best is None else jnp.maximum(best, values)
    s_ref[...] = jnp.max(best, axis=0, keepdims=True)


def whiten_and_score(x, inv, queries, scale):
    rows, width = x.shape
    tile = 512
    whitened, scores = pl.pallas_call(
        functools.partial(score_kernel, scale, 512),
        grid=(rows // tile,),
        out_shape=(
            jax.ShapeDtypeStruct((rows, width), jnp.float32),
            jax.ShapeDtypeStruct((1, rows), jnp.float32),
        ),
        in_specs=[pl.BlockSpec((tile, width), lambda i: (i, 0)), VMEM] + [VMEM] * len(queries),
        out_specs=(
            pl.BlockSpec((tile, width), lambda i: (i, 0)),
            pl.BlockSpec((1, tile), lambda i: (0, i)),
        ),
        scratch_shapes=[pltpu.VMEM((width, width), jnp.bfloat16)] * 2,
        compiler_params=pltpu.CompilerParams(vmem_limit_bytes=48 << 20),
        name="score",
    )(x, inv, *queries)
    return whitened, scores.reshape(rows)


def solution(mesh):
    fine = Mesh(mesh.devices.reshape(2, 4, 2, 4, 4), FINE)
    placed = (P(FINE, None), P(("y", "z_hi"), None))
    return jax.shard_map(
        body, mesh=fine, in_specs=placed, out_specs=(P(FINE, None), P(FINE)), check_vma=False
    )
```

```python
import functools
import itertools

import jax
import jax.numpy as jnp
from jax import lax
from jax.experimental import pallas as pl
from jax.experimental.pallas import tpu as pltpu
from jax.sharding import Mesh, PartitionSpec as P

FINE = ("z_lo", "x", "core", "y", "z_hi")
B = 128
SWAP = [(0, 1), (1, 0)]
W = 16
VMEM = pl.BlockSpec(memory_space=pltpu.VMEM)
SMEM = pl.BlockSpec(memory_space=pltpu.SMEM)


def exact_dot(a, b, dims):
    return lax.dot_general(
        a, b, (dims, ((), ())), precision=lax.Precision.HIGHEST, preferred_element_type=jnp.float32
    )


def gram_kernel(core_ref, x_ref, mine_ref, other_ref, packed):
    width = x_ref.shape[1]
    count = width // B
    at = 0
    for i in range(0, count, 2):
        left = x_ref[:, i * B : (i + 2) * B]
        part = lax.dot_general(
            left, x_ref[:, i * B :], (((0,), (0,)), ((), ())), preferred_element_type=jnp.float32
        )
        for r in range(2):
            for j in range(i + r, count):
                packed[at * B : (at + 1) * B, :] = part[r * B : (r + 1) * B, (j - i) * B : (j - i + 1) * B]
                at += 1
    half = mine_ref.shape[0]
    core = core_ref[0]
    mine_ref[...] = packed[pl.ds(pl.multiple_of(core * half, 8), half), :]
    other_ref[...] = packed[pl.ds(pl.multiple_of((1 - core) * half, 8), half), :]


def local_gram(core, x):
    count = x.shape[1] // B
    rows = count * (count + 1) // 2 * B
    half = jax.ShapeDtypeStruct((rows // 2, B), jnp.float32)
    return pl.pallas_call(
        gram_kernel,
        out_shape=(half, half),
        in_specs=[SMEM, VMEM],
        out_specs=(VMEM, VMEM),
        scratch_shapes=[pltpu.VMEM((rows, B), jnp.float32)],
        compiler_params=pltpu.CompilerParams(vmem_limit_bytes=16 << 20),
        name="gram",
    )(core, x)


def spread(x, lane):
    return jnp.take_along_axis(x, jnp.full(x.shape, lane, jnp.int32), axis=1)


def tree_sum(terms):
    terms = list(terms)
    while len(terms) > 1:
        pairs = [a + b for a, b in zip(terms[::2], terms[1::2])]
        terms = pairs + terms[len(pairs) * 2 :]
    return terms[0]


def gram_of_rows(s):
    high = s.astype(jnp.bfloat16)
    rest = s - high.astype(jnp.float32)
    mid = rest.astype(jnp.bfloat16)
    low = (rest - mid.astype(jnp.float32)).astype(jnp.bfloat16)
    return lax.dot_general(
        jnp.concatenate([high, high, mid, high, low, mid], 0),
        jnp.concatenate([high, mid, high, low, high, mid], 0),
        (((0,), (0,)), ((), ())),
        preferred_element_type=jnp.float32,
    )


def eliminate(a):
    n = a.shape[0]
    panels = n // W
    lane = lax.broadcasted_iota(jnp.int32, (W, n), 1)
    sub = lax.broadcasted_iota(jnp.int32, (W, n), 0)

    def row(x, j):
        return jnp.broadcast_to(x[j : j + 1], (W, n))

    out = []
    groups = [a[p * W : (p + 1) * W] for p in range(panels)]
    for p in range(panels):
        c = p * W
        here = (lane >= c) & (lane < c + W)
        cols = [spread(groups[p], c + k) for k in range(W)]
        low = jnp.where(here, jnp.where(lane - c == sub, 1.0, 0.0), groups[p])
        full = low
        inverse = jnp.ones((W, n), jnp.float32)
        for j in range(W):
            one = 1.0 / row(cols[j], j)
            ratio = jnp.where(sub == j, 0.0, cols[j] * one)
            inverse = jnp.where(sub == j, one, inverse)
            for k in range(j + 1, W):
                cols[k] = cols[k] - ratio * row(cols[k], j)
            full = full - ratio * row(full, j)
            low = low - jnp.where(sub > j, ratio, 0.0) * row(low, j)
        low = low * (lax.rsqrt(inverse) * inverse)
        out.append(jnp.where(lane < c + W, low, 0.0))
        if p < panels - 1:
            full = full * inverse
            near = tree_sum(spread(groups[p + 1], c + k) * row(full, k) for k in range(W))
            groups[p + 1] = jnp.where(here, 0.0, groups[p + 1]) - near
            if p < panels - 2:
                far = gram_of_rows(low)
                for g in range(p + 2, panels):
                    groups[g] = jnp.where(here, 0.0, groups[g]) - far[g * W : (g + 1) * W]
    return jnp.concatenate(out, 0)


def factor_step(k, count, state, top, put):
    def rows(i):
        return slice((i - top) * B, (i - top + 1) * B)

    r, c = rows(k), slice(k * B, (k + 1) * B)
    inv = eliminate(state[r, c])
    left = inv
    if k > 0:
        left = jnp.concatenate([exact_dot(inv, state[r, : k * B], ((1,), (0,))), inv], 1)
    if k == count - 1:
        put(left)
        return
    put(jnp.concatenate([left, jnp.zeros((B, (count - 1 - k) * B), jnp.float32)], 1))
    right = exact_dot(inv, state[r, (k + 1) * B :], ((1,), (0,)))
    for i in range(k + 1, count):
        ri = rows(i)
        coef = right[:, (i - k - 1) * B : (i - k) * B]
        state[ri, i * B :] = state[ri, i * B :] - exact_dot(coef, right[:, (i - k - 1) * B :], ((0,), (0,)))
        new = exact_dot(coef, left, ((0,), (0,)))
        if k > 0:
            state[ri, : k * B] = state[ri, : k * B] - new[:, : k * B]
        state[ri, c] = -new[:, k * B :]


def first_kernel(core_ref, mine_ref, other_ref, o_ref, last_ref, packed, state):
    half = mine_ref.shape[0]
    core = core_ref[0]
    packed[pl.ds(pl.multiple_of(core * half, 8), half), :] = mine_ref[...]
    packed[pl.ds(pl.multiple_of((1 - core) * half, 8), half), :] = other_ref[...]
    count = o_ref.shape[1] // B
    at = 0
    for i in range(count):
        for j in range(i, count):
            state[i * B : (i + 1) * B, j * B : (j + 1) * B] = packed[at * B : (at + 1) * B, :]
            at += 1
    for k in range(count - 1):

        def put(value, k=k):
            o_ref[k * B : (k + 1) * B, :] = value

        factor_step(k, count, state, 0, put)
    last_ref[...] = state[(count - 1) * B :, :]


def last_kernel(state_ref, o_ref):
    count = o_ref.shape[1] // B

    def put(value):
        o_ref[...] = value

    factor_step(count - 1, count, state_ref, count - 1, put)


def first_rows(core, mine, other, n):
    return pl.pallas_call(
        first_kernel,
        out_shape=(jax.ShapeDtypeStruct((n - B, n), jnp.float32), jax.ShapeDtypeStruct((B, n), jnp.float32)),
        in_specs=[SMEM, VMEM, VMEM],
        out_specs=(VMEM, VMEM),
        scratch_shapes=[pltpu.VMEM((2 * mine.shape[0], B), jnp.float32), pltpu.VMEM((n, n), jnp.float32)],
        compiler_params=pltpu.CompilerParams(vmem_limit_bytes=16 << 20),
        name="factor",
    )(core, mine, other)


def last_rows(state):
    return pl.pallas_call(
        last_kernel,
        out_shape=jax.ShapeDtypeStruct(state.shape, jnp.float32),
        in_specs=[VMEM],
        out_specs=VMEM,
        compiler_params=pltpu.CompilerParams(vmem_limit_bytes=16 << 20),
        name="factor_end",
    )(state)


def steps(move):
    shape = [lax.axis_size(axis) for axis in FINE]
    places = list(itertools.product(*map(range, shape)))
    number = {place: i for i, place in enumerate(places)}
    length = max(n for place in places for n, by in zip(shape, move(place)) if by)

    def source(place, k):
        return number[tuple((at + k * by) % n for at, by, n in zip(place, move(place), shape))]

    return [[(source(place, k), number[place]) for place in places] for k in range(1, length)]


def gather(own, move):
    return [own] + [lax.ppermute(own, FINE, step) for step in steps(move)]


def along_z(place):
    return (0, 0, 0, 0, 1)


def along_one(place):
    return (0, 1, 0, 0, 0) if place[2] else (0, 0, 0, 1, 0)


def along_other(place):
    return (0, 0, 0, 1, 0) if place[2] else (0, 1, 0, 0, 0)


def body(examples, queries):
    rows, width = examples.shape
    plane = lax.axis_size("x") * lax.axis_size("y")
    depth = lax.axis_size("z_lo") * lax.axis_size("z_hi")
    index = lax.axis_index("core").astype(jnp.int32)
    share = queries.shape[0] // (2 * lax.axis_size("x"))
    start = (index * lax.axis_size("x") + lax.axis_index("x")) * share
    piece = lax.dynamic_slice_in_dim(queries, start, share, 0)
    pieces = gather(piece, along_z)

    core = index.reshape(1)
    mine, other = local_gram(core, examples)
    mine = mine + lax.ppermute(other, "core", SWAP)
    part = jnp.sum(lax.all_to_all(mine.reshape(plane, -1, B), ("x", "y"), 0, 0), 0)

    pieces, part = lax.optimization_barrier((pieces, part))
    pieces = gather(jnp.concatenate(pieces, 0), along_one)

    spread = jnp.broadcast_to(part[None], (depth, *part.shape))
    part = jnp.sum(lax.all_to_all(spread, ("z_lo", "z_hi"), 0, 0), 0)

    pieces, part = lax.optimization_barrier((pieces, part))
    pieces = gather(jnp.concatenate(pieces, 0), along_other)

    spread = jnp.broadcast_to(part[None], (plane, *part.shape))
    mine = lax.all_to_all(spread, ("x", "y"), 0, 0).reshape(mine.shape)
    other = lax.ppermute(mine, "core", SWAP)
    top, last = first_rows(core, mine, other, width)

    pieces, last = lax.optimization_barrier((pieces, last))
    pieces = pieces + [lax.ppermute(p, "core", SWAP) for p in pieces]
    end = last_rows(last)
    count = rows
    for axis in FINE:
        count *= lax.axis_size(axis)
    return whiten_and_score(examples, top, end, pieces, float(count) ** 0.5)


def score_kernel(scale, tile, step, x_ref, top_ref, end_ref, *refs):
    *q_refs, w_hbm, s_ref, high, low, w_ref, r_ref, sent = refs
    n = high.shape[0]
    for at, part in ((0, top_ref[...]), (n - B, end_ref[...])):
        rows = slice(at, at + part.shape[0])
        part = part * scale
        head = part.astype(jnp.bfloat16)
        high[rows, :] = head
        low[rows, :] = (part - head.astype(jnp.float32)).astype(jnp.bfloat16)
    dims = (((1,), (1,)), ((), ()))
    wide = 2 * B
    copies = []
    for t in range(0, x_ref.shape[0], tile):
        x = x_ref[t : t + tile, :]
        for at in range(0, n, wide):
            end = at + wide
            part = lax.dot_general(
                x[:, :end], high[at:end, :end], dims, preferred_element_type=jnp.float32
            ) + lax.dot_general(x[:, :end], low[at:end, :end], dims, preferred_element_type=jnp.float32)
            w_ref[t : t + tile, at:end] = part
            r_ref[t : t + tile, at:end] = part.astype(jnp.bfloat16)
        here = pl.ds(t, tile)
        copies.append(pltpu.make_async_copy(w_ref.at[here], w_hbm.at[here], sent.at[t // tile]))
        copies[-1].start()
    rounded = r_ref[...]
    best = None
    for q_ref in q_refs:
        for m in range(0, q_ref.shape[0], step):
            values = lax.dot_general(
                q_ref[m : m + step, :], rounded, dims, preferred_element_type=jnp.float32
            )
            values = jnp.max(values.reshape(step // 8, 8, values.shape[1]), axis=0)
            best = values if best is None else jnp.maximum(best, values)
    s_ref[...] = jnp.max(best, axis=0, keepdims=True)
    for copy in copies:
        copy.wait()


def whiten_and_score(x, top, end, queries, scale):
    rows, width = x.shape
    tile = 256
    whitened, scores = pl.pallas_call(
        functools.partial(score_kernel, scale, tile, 256),
        out_shape=(
            jax.ShapeDtypeStruct((rows, width), jnp.float32),
            jax.ShapeDtypeStruct((1, rows), jnp.float32),
        ),
        in_specs=[VMEM] * (3 + len(queries)),
        out_specs=(pl.BlockSpec(memory_space=pl.ANY), VMEM),
        scratch_shapes=[
            pltpu.VMEM((width, width), jnp.bfloat16),
            pltpu.VMEM((width, width), jnp.bfloat16),
            pltpu.VMEM((rows, width), jnp.float32),
            pltpu.VMEM((rows, width), jnp.bfloat16),
            pltpu.SemaphoreType.DMA((rows // tile,)),
        ],
        compiler_params=pltpu.CompilerParams(vmem_limit_bytes=24 << 20),
        name="score",
    )(x, top, end, *queries)
    return whitened, scores.reshape(rows)


def solution(mesh):
    fine = Mesh(mesh.devices.reshape(2, 4, 2, 4, 4), FINE)
    placed = (P(FINE, None), P(("y", "z_hi"), None))
    return jax.shard_map(
        body, mesh=fine, in_specs=placed, out_specs=(P(FINE, None), P(FINE)), check_vma=False
    )
```

```python
import functools
import itertools

import jax
import jax.numpy as jnp
from jax import lax
from jax.experimental import pallas as pl
from jax.experimental.pallas import tpu as pltpu
from jax.sharding import Mesh, PartitionSpec as P

FINE = ("z_lo", "x", "core", "y", "z_hi")
B = 128
SWAP = [(0, 1), (1, 0)]
W = 16
VMEM = pl.BlockSpec(memory_space=pltpu.VMEM)
SMEM = pl.BlockSpec(memory_space=pltpu.SMEM)


def exact_dot(a, b, dims):
    return lax.dot_general(
        a, b, (dims, ((), ())), precision=lax.Precision.HIGHEST, preferred_element_type=jnp.float32
    )


def gram_kernel(core_ref, x_ref, mine_ref, other_ref, packed):
    width = x_ref.shape[1]
    count = width // B
    at = 0
    for i in range(0, count, 2):
        left = x_ref[:, i * B : (i + 2) * B]
        part = lax.dot_general(
            left, x_ref[:, i * B :], (((0,), (0,)), ((), ())), preferred_element_type=jnp.float32
        )
        for r in range(2):
            for j in range(i + r, count):
                packed[at * B : (at + 1) * B, :] = part[r * B : (r + 1) * B, (j - i) * B : (j - i + 1) * B]
                at += 1
    half = mine_ref.shape[0]
    core = core_ref[0]
    mine_ref[...] = packed[pl.ds(pl.multiple_of(core * half, 8), half), :]
    other_ref[...] = packed[pl.ds(pl.multiple_of((1 - core) * half, 8), half), :]


def local_gram(core, x):
    count = x.shape[1] // B
    rows = count * (count + 1) // 2 * B
    half = jax.ShapeDtypeStruct((rows // 2, B), jnp.float32)
    return pl.pallas_call(
        gram_kernel,
        out_shape=(half, half),
        in_specs=[SMEM, VMEM],
        out_specs=(VMEM, VMEM),
        scratch_shapes=[pltpu.VMEM((rows, B), jnp.float32)],
        compiler_params=pltpu.CompilerParams(vmem_limit_bytes=16 << 20),
        name="gram",
    )(core, x)


def spread(x, lane):
    return jnp.take_along_axis(x, jnp.full(x.shape, lane, jnp.int32), axis=1)


def tree_sum(terms):
    terms = list(terms)
    while len(terms) > 1:
        pairs = [a + b for a, b in zip(terms[::2], terms[1::2])]
        terms = pairs + terms[len(pairs) * 2 :]
    return terms[0]


def gram_of_rows(s):
    high = s.astype(jnp.bfloat16)
    rest = s - high.astype(jnp.float32)
    mid = rest.astype(jnp.bfloat16)
    low = (rest - mid.astype(jnp.float32)).astype(jnp.bfloat16)
    return lax.dot_general(
        jnp.concatenate([high, high, mid, high, low, mid], 0),
        jnp.concatenate([high, mid, high, low, high, mid], 0),
        (((0,), (0,)), ((), ())),
        preferred_element_type=jnp.float32,
    )


def eliminate(a):
    n = a.shape[0]
    panels = n // W
    lane = lax.broadcasted_iota(jnp.int32, (W, n), 1)
    sub = lax.broadcasted_iota(jnp.int32, (W, n), 0)

    def row(x, j):
        return jnp.broadcast_to(x[j : j + 1], (W, n))

    out = []
    groups = [a[p * W : (p + 1) * W] for p in range(panels)]
    for p in range(panels):
        c = p * W
        here = (lane >= c) & (lane < c + W)
        cols = [spread(groups[p], c + k) for k in range(W)]
        low = jnp.where(here, jnp.where(lane - c == sub, 1.0, 0.0), groups[p])
        full = low
        inverse = jnp.ones((W, n), jnp.float32)
        for j in range(W):
            one = 1.0 / row(cols[j], j)
            ratio = jnp.where(sub == j, 0.0, cols[j] * one)
            inverse = jnp.where(sub == j, one, inverse)
            for k in range(j + 1, W):
                cols[k] = cols[k] - ratio * row(cols[k], j)
            full = full - ratio * row(full, j)
            low = low - jnp.where(sub > j, ratio, 0.0) * row(low, j)
        low = low * (lax.rsqrt(inverse) * inverse)
        out.append(jnp.where(lane < c + W, low, 0.0))
        if p < panels - 1:
            full = full * inverse
            near = tree_sum(spread(groups[p + 1], c + k) * row(full, k) for k in range(W))
            groups[p + 1] = jnp.where(here, 0.0, groups[p + 1]) - near
            if p < panels - 2:
                far = gram_of_rows(low)
                for g in range(p + 2, panels):
                    groups[g] = jnp.where(here, 0.0, groups[g]) - far[g * W : (g + 1) * W]
    return jnp.concatenate(out, 0)


def factor_step(k, count, state, top, put):
    def rows(i):
        return slice((i - top) * B, (i - top + 1) * B)

    r, c = rows(k), slice(k * B, (k + 1) * B)
    inv = eliminate(state[r, c])
    left = inv
    if k > 0:
        left = jnp.concatenate([exact_dot(inv, state[r, : k * B], ((1,), (0,))), inv], 1)
    if k == count - 1:
        put(left)
        return
    put(jnp.concatenate([left, jnp.zeros((B, (count - 1 - k) * B), jnp.float32)], 1))
    right = exact_dot(inv, state[r, (k + 1) * B :], ((1,), (0,)))
    for i in range(k + 1, count):
        ri = rows(i)
        coef = right[:, (i - k - 1) * B : (i - k) * B]
        state[ri, i * B :] = state[ri, i * B :] - exact_dot(coef, right[:, (i - k - 1) * B :], ((0,), (0,)))
        new = exact_dot(coef, left, ((0,), (0,)))
        if k > 0:
            state[ri, : k * B] = state[ri, : k * B] - new[:, : k * B]
        state[ri, c] = -new[:, k * B :]


def first_kernel(core_ref, mine_ref, other_ref, o_ref, last_ref, packed, state):
    half = mine_ref.shape[0]
    core = core_ref[0]
    packed[pl.ds(pl.multiple_of(core * half, 8), half), :] = mine_ref[...]
    packed[pl.ds(pl.multiple_of((1 - core) * half, 8), half), :] = other_ref[...]
    count = o_ref.shape[1] // B
    at = 0
    for i in range(count):
        for j in range(i, count):
            state[i * B : (i + 1) * B, j * B : (j + 1) * B] = packed[at * B : (at + 1) * B, :]
            at += 1
    for k in range(count - 1):

        def put(value, k=k):
            o_ref[k * B : (k + 1) * B, :] = value

        factor_step(k, count, state, 0, put)
    last_ref[...] = state[(count - 1) * B :, :]


def last_kernel(state_ref, o_ref):
    count = o_ref.shape[1] // B

    def put(value):
        o_ref[...] = value

    factor_step(count - 1, count, state_ref, count - 1, put)


def first_rows(core, mine, other, n):
    return pl.pallas_call(
        first_kernel,
        out_shape=(jax.ShapeDtypeStruct((n - B, n), jnp.float32), jax.ShapeDtypeStruct((B, n), jnp.float32)),
        in_specs=[SMEM, VMEM, VMEM],
        out_specs=(VMEM, VMEM),
        scratch_shapes=[pltpu.VMEM((2 * mine.shape[0], B), jnp.float32), pltpu.VMEM((n, n), jnp.float32)],
        compiler_params=pltpu.CompilerParams(vmem_limit_bytes=16 << 20),
        name="factor",
    )(core, mine, other)


def last_rows(state):
    return pl.pallas_call(
        last_kernel,
        out_shape=jax.ShapeDtypeStruct(state.shape, jnp.float32),
        in_specs=[VMEM],
        out_specs=VMEM,
        compiler_params=pltpu.CompilerParams(vmem_limit_bytes=16 << 20),
        name="factor_end",
    )(state)


def steps(move):
    shape = [lax.axis_size(axis) for axis in FINE]
    places = list(itertools.product(*map(range, shape)))
    number = {place: i for i, place in enumerate(places)}
    length = max(n for place in places for n, by in zip(shape, move(place)) if by)

    def source(place, k):
        return number[tuple((at + k * by) % n for at, by, n in zip(place, move(place), shape))]

    return [[(source(place, k), number[place]) for place in places] for k in range(1, length)]


def gather(own, move):
    return [own] + [lax.ppermute(own, FINE, step) for step in steps(move)]


def along_z():
    shape = [lax.axis_size(axis) for axis in FINE]
    places = list(itertools.product(*map(range, shape)))
    number = {place: i for i, place in enumerate(places)}

    def source(place, by):
        return number[(*place[:4], (place[4] + by) % shape[4])]

    return (
        [(source(place, -1 if place[2] else 1), number[place]) for place in places],
        [(source(place, 2), number[place]) for place in places if place[2]],
    )


def along_one(place):
    return (0, 1, 0, 0, 0) if place[2] else (0, 0, 0, 1, 0)


def along_other(place):
    return (0, 0, 0, 1, 0) if place[2] else (0, 1, 0, 0, 0)


def body(examples, queries):
    rows, width = examples.shape
    plane = lax.axis_size("x") * lax.axis_size("y")
    depth = lax.axis_size("z_lo") * lax.axis_size("z_hi")
    index = lax.axis_index("core").astype(jnp.int32)
    share = queries.shape[0] // lax.axis_size("x")
    piece = lax.dynamic_slice_in_dim(queries, lax.axis_index("x") * share, share, 0)
    beside, across = (lax.ppermute(piece, FINE, step) for step in along_z())
    pieces = [jnp.where(index == 0, piece, across), beside]

    core = index.reshape(1)
    mine, other = local_gram(core, examples)
    mine = mine + lax.ppermute(other, "core", SWAP)
    part = jnp.sum(lax.all_to_all(mine.reshape(plane, -1, B), ("x", "y"), 0, 0), 0)

    pieces, part = lax.optimization_barrier((pieces, part))
    pieces = gather(jnp.concatenate(pieces, 0), along_one)

    spread = jnp.broadcast_to(part[None], (depth, *part.shape))
    part = jnp.sum(lax.all_to_all(spread, ("z_lo", "z_hi"), 0, 0), 0)

    pieces, part = lax.optimization_barrier((pieces, part))
    pieces = gather(jnp.concatenate(pieces, 0), along_other)

    spread = jnp.broadcast_to(part[None], (plane, *part.shape))
    mine = lax.all_to_all(spread, ("x", "y"), 0, 0).reshape(mine.shape)
    other = lax.ppermute(mine, "core", SWAP)
    top, last = first_rows(core, mine, other, width)

    pieces, last = lax.optimization_barrier((pieces, last))
    pieces = pieces + [lax.ppermute(p, "core", SWAP) for p in pieces]
    end = last_rows(last)
    count = rows
    for axis in FINE:
        count *= lax.axis_size(axis)
    return whiten_and_score(examples, top, end, pieces, float(count) ** 0.5)


def score_kernel(scale, tile, step, x_ref, top_ref, end_ref, *refs):
    *q_refs, w_hbm, s_ref, high, low, w_ref, r_ref, sent = refs
    n = high.shape[0]
    for at, part in ((0, top_ref[...]), (n - B, end_ref[...])):
        rows = slice(at, at + part.shape[0])
        part = part * scale
        head = part.astype(jnp.bfloat16)
        high[rows, :] = head
        low[rows, :] = (part - head.astype(jnp.float32)).astype(jnp.bfloat16)
    dims = (((1,), (1,)), ((), ()))
    wide = 2 * B
    copies = []
    for t in range(0, x_ref.shape[0], tile):
        x = x_ref[t : t + tile, :]
        for at in range(0, n, wide):
            end = at + wide
            part = lax.dot_general(
                x[:, :end], high[at:end, :end], dims, preferred_element_type=jnp.float32
            ) + lax.dot_general(x[:, :end], low[at:end, :end], dims, preferred_element_type=jnp.float32)
            w_ref[t : t + tile, at:end] = part
            r_ref[t : t + tile, at:end] = part.astype(jnp.bfloat16)
        here = pl.ds(t, tile)
        copies.append(pltpu.make_async_copy(w_ref.at[here], w_hbm.at[here], sent.at[t // tile]))
        copies[-1].start()
    rounded = r_ref[...]
    best = None
    for q_ref in q_refs:
        for m in range(0, q_ref.shape[0], step):
            values = lax.dot_general(
                q_ref[m : m + step, :], rounded, dims, preferred_element_type=jnp.float32
            )
            values = jnp.max(values.reshape(step // 8, 8, values.shape[1]), axis=0)
            best = values if best is None else jnp.maximum(best, values)
    s_ref[...] = jnp.max(best, axis=0, keepdims=True)
    for copy in copies:
        copy.wait()


def whiten_and_score(x, top, end, queries, scale):
    rows, width = x.shape
    tile = 256
    whitened, scores = pl.pallas_call(
        functools.partial(score_kernel, scale, tile, 256),
        out_shape=(
            jax.ShapeDtypeStruct((rows, width), jnp.float32),
            jax.ShapeDtypeStruct((1, rows), jnp.float32),
        ),
        in_specs=[VMEM] * (3 + len(queries)),
        out_specs=(pl.BlockSpec(memory_space=pl.ANY), VMEM),
        scratch_shapes=[
            pltpu.VMEM((width, width), jnp.bfloat16),
            pltpu.VMEM((width, width), jnp.bfloat16),
            pltpu.VMEM((rows, width), jnp.float32),
            pltpu.VMEM((rows, width), jnp.bfloat16),
            pltpu.SemaphoreType.DMA((rows // tile,)),
        ],
        compiler_params=pltpu.CompilerParams(vmem_limit_bytes=24 << 20),
        name="score",
    )(x, top, end, *queries)
    return whitened, scores.reshape(rows)


def solution(mesh):
    fine = Mesh(mesh.devices.reshape(2, 4, 2, 4, 4), FINE)
    placed = (P(FINE, None), P(("y", "z_hi"), None))
    return jax.shard_map(
        body, mesh=fine, in_specs=placed, out_specs=(P(FINE, None), P(FINE)), check_vma=False
    )
```

```python
import functools
import itertools

import jax
import jax.numpy as jnp
from jax import lax
from jax.experimental import pallas as pl
from jax.experimental.pallas import tpu as pltpu
from jax.sharding import Mesh, PartitionSpec as P

FINE = ("z_lo", "x", "core", "y", "z_hi")
B = 128
SWAP = [(0, 1), (1, 0)]
W = 16
VMEM = pl.BlockSpec(memory_space=pltpu.VMEM)
SMEM = pl.BlockSpec(memory_space=pltpu.SMEM)


def exact_dot(a, b, dims):
    return lax.dot_general(
        a, b, (dims, ((), ())), precision=lax.Precision.HIGHEST, preferred_element_type=jnp.float32
    )


def gram_kernel(core_ref, x_ref, mine_ref, other_ref, packed):
    width = x_ref.shape[1]
    count = width // B
    at = 0
    for i in range(0, count, 2):
        left = x_ref[:, i * B : (i + 2) * B]
        part = lax.dot_general(
            left, x_ref[:, i * B :], (((0,), (0,)), ((), ())), preferred_element_type=jnp.float32
        )
        for r in range(2):
            for j in range(i + r, count):
                packed[at * B : (at + 1) * B, :] = part[r * B : (r + 1) * B, (j - i) * B : (j - i + 1) * B]
                at += 1
    half = mine_ref.shape[0]
    core = core_ref[0]
    mine_ref[...] = packed[pl.ds(pl.multiple_of(core * half, 8), half), :]
    other_ref[...] = packed[pl.ds(pl.multiple_of((1 - core) * half, 8), half), :]


def local_gram(core, x):
    count = x.shape[1] // B
    rows = count * (count + 1) // 2 * B
    half = jax.ShapeDtypeStruct((rows // 2, B), jnp.float32)
    return pl.pallas_call(
        gram_kernel,
        out_shape=(half, half),
        in_specs=[SMEM, VMEM],
        out_specs=(VMEM, VMEM),
        scratch_shapes=[pltpu.VMEM((rows, B), jnp.float32)],
        compiler_params=pltpu.CompilerParams(vmem_limit_bytes=16 << 20),
        name="gram",
    )(core, x)


def spread(x, lane):
    return jnp.take_along_axis(x, jnp.full(x.shape, lane, jnp.int32), axis=1)


def tree_sum(terms):
    terms = list(terms)
    while len(terms) > 1:
        pairs = [a + b for a, b in zip(terms[::2], terms[1::2])]
        terms = pairs + terms[len(pairs) * 2 :]
    return terms[0]


def gram_of_rows(s):
    high = s.astype(jnp.bfloat16)
    rest = s - high.astype(jnp.float32)
    mid = rest.astype(jnp.bfloat16)
    low = (rest - mid.astype(jnp.float32)).astype(jnp.bfloat16)
    return lax.dot_general(
        jnp.concatenate([high, high, mid, high, low, mid], 0),
        jnp.concatenate([high, mid, high, low, high, mid], 0),
        (((0,), (0,)), ((), ())),
        preferred_element_type=jnp.float32,
    )


def eliminate(a):
    n = a.shape[0]
    panels = n // W
    lane = lax.broadcasted_iota(jnp.int32, (W, n), 1)
    sub = lax.broadcasted_iota(jnp.int32, (W, n), 0)

    def row(x, j):
        return jnp.broadcast_to(x[j : j + 1], (W, n))

    out = []
    groups = [a[p * W : (p + 1) * W] for p in range(panels)]
    for p in range(panels):
        c = p * W
        here = (lane >= c) & (lane < c + W)
        cols = [spread(groups[p], c + k) for k in range(W)]
        low = jnp.where(here, jnp.where(lane - c == sub, 1.0, 0.0), groups[p])
        full = low
        inverse = jnp.ones((W, n), jnp.float32)
        for j in range(W):
            one = 1.0 / row(cols[j], j)
            ratio = jnp.where(sub == j, 0.0, cols[j] * one)
            inverse = jnp.where(sub == j, one, inverse)
            for k in range(j + 1, W):
                cols[k] = cols[k] - ratio * row(cols[k], j)
            full = full - ratio * row(full, j)
            low = low - jnp.where(sub > j, ratio, 0.0) * row(low, j)
        low = low * (lax.rsqrt(inverse) * inverse)
        out.append(jnp.where(lane < c + W, low, 0.0))
        if p < panels - 1:
            full = full * inverse
            near = tree_sum(spread(groups[p + 1], c + k) * row(full, k) for k in range(W))
            groups[p + 1] = jnp.where(here, 0.0, groups[p + 1]) - near
            if p < panels - 2:
                far = gram_of_rows(low)
                for g in range(p + 2, panels):
                    groups[g] = jnp.where(here, 0.0, groups[g]) - far[g * W : (g + 1) * W]
    return jnp.concatenate(out, 0)


def factor_step(k, count, state, top, put):
    def rows(i):
        return slice((i - top) * B, (i - top + 1) * B)

    def cols(j):
        return slice(j * B, (j + 1) * B)

    inv = eliminate(state[rows(k), cols(k)])
    right = {}
    for j in range(k + 1, count):
        right[j] = exact_dot(inv, state[rows(k), cols(j)], ((1,), (0,)))
        if j == k + 1:
            state[rows(j), cols(j)] = state[rows(j), cols(j)] - exact_dot(right[j], right[j], ((0,), (0,)))
    left = inv
    if k > 0:
        left = jnp.concatenate([exact_dot(inv, state[rows(k), : k * B], ((1,), (0,))), inv], 1)
    if k == count - 1:
        put(left)
        return
    put(jnp.concatenate([left, jnp.zeros((B, (count - 1 - k) * B), jnp.float32)], 1))
    for i in range(k + 1, count):
        for j in range(i, count):
            if j > k + 1:
                state[rows(i), cols(j)] = state[rows(i), cols(j)] - exact_dot(right[i], right[j], ((0,), (0,)))
        new = exact_dot(right[i], left, ((0,), (0,)))
        if k > 0:
            state[rows(i), : k * B] = state[rows(i), : k * B] - new[:, : k * B]
        state[rows(i), cols(k)] = -new[:, k * B :]


def first_kernel(core_ref, mine_ref, other_ref, o_ref, last_ref, packed, state):
    half = mine_ref.shape[0]
    core = core_ref[0]
    packed[pl.ds(pl.multiple_of(core * half, 8), half), :] = mine_ref[...]
    packed[pl.ds(pl.multiple_of((1 - core) * half, 8), half), :] = other_ref[...]
    count = o_ref.shape[1] // B
    at = 0
    for i in range(count):
        for j in range(i, count):
            state[i * B : (i + 1) * B, j * B : (j + 1) * B] = packed[at * B : (at + 1) * B, :]
            at += 1
    for k in range(count - 1):

        def put(value, k=k):
            o_ref[k * B : (k + 1) * B, :] = value

        factor_step(k, count, state, 0, put)
    last_ref[...] = state[(count - 1) * B :, :]


def last_kernel(state_ref, o_ref):
    count = o_ref.shape[1] // B

    def put(value):
        o_ref[...] = value

    factor_step(count - 1, count, state_ref, count - 1, put)


def first_rows(core, mine, other, n):
    return pl.pallas_call(
        first_kernel,
        out_shape=(jax.ShapeDtypeStruct((n - B, n), jnp.float32), jax.ShapeDtypeStruct((B, n), jnp.float32)),
        in_specs=[SMEM, VMEM, VMEM],
        out_specs=(VMEM, VMEM),
        scratch_shapes=[pltpu.VMEM((2 * mine.shape[0], B), jnp.float32), pltpu.VMEM((n, n), jnp.float32)],
        compiler_params=pltpu.CompilerParams(vmem_limit_bytes=16 << 20),
        name="factor",
    )(core, mine, other)


def last_rows(state):
    return pl.pallas_call(
        last_kernel,
        out_shape=jax.ShapeDtypeStruct(state.shape, jnp.float32),
        in_specs=[VMEM],
        out_specs=VMEM,
        compiler_params=pltpu.CompilerParams(vmem_limit_bytes=16 << 20),
        name="factor_end",
    )(state)


def steps(move):
    shape = [lax.axis_size(axis) for axis in FINE]
    places = list(itertools.product(*map(range, shape)))
    number = {place: i for i, place in enumerate(places)}
    length = max(n for place in places for n, by in zip(shape, move(place)) if by)

    def source(place, k):
        return number[tuple((at + k * by) % n for at, by, n in zip(place, move(place), shape))]

    return [[(source(place, k), number[place]) for place in places] for k in range(1, length)]


def gather(own, move):
    return [own] + [lax.ppermute(own, FINE, step) for step in steps(move)]


def along_z():
    shape = [lax.axis_size(axis) for axis in FINE]
    places = list(itertools.product(*map(range, shape)))
    number = {place: i for i, place in enumerate(places)}

    def source(place, by):
        return number[(*place[:4], (place[4] + by) % shape[4])]

    return (
        [(source(place, -1 if place[2] else 1), number[place]) for place in places],
        [(source(place, 2), number[place]) for place in places if place[2]],
    )


def along_one(place):
    return (0, 1, 0, 0, 0) if place[2] else (0, 0, 0, 1, 0)


def along_other(place):
    return (0, 0, 0, 1, 0) if place[2] else (0, 1, 0, 0, 0)


def body(examples, queries):
    rows, width = examples.shape
    plane = lax.axis_size("x") * lax.axis_size("y")
    depth = lax.axis_size("z_lo") * lax.axis_size("z_hi")
    index = lax.axis_index("core").astype(jnp.int32)
    share = queries.shape[0] // lax.axis_size("x")
    piece = lax.dynamic_slice_in_dim(queries, lax.axis_index("x") * share, share, 0)
    beside, across = (lax.ppermute(piece, FINE, step) for step in along_z())
    pieces = [jnp.where(index == 0, piece, across), beside]

    core = index.reshape(1)
    mine, other = local_gram(core, examples)
    mine = mine + lax.ppermute(other, "core", SWAP)
    part = jnp.sum(lax.all_to_all(mine.reshape(plane, -1, B), ("x", "y"), 0, 0), 0)

    pieces, part = lax.optimization_barrier((pieces, part))
    pieces = gather(jnp.concatenate(pieces, 0), along_one)

    spread = jnp.broadcast_to(part[None], (depth, *part.shape))
    part = jnp.sum(lax.all_to_all(spread, ("z_lo", "z_hi"), 0, 0), 0)

    pieces, part = lax.optimization_barrier((pieces, part))
    pieces = gather(jnp.concatenate(pieces, 0), along_other)
    swapped = [lax.ppermute(pieces[0], "core", SWAP)]

    spread = jnp.broadcast_to(part[None], (plane, *part.shape))
    mine = lax.all_to_all(spread, ("x", "y"), 0, 0).reshape(mine.shape)
    other = lax.ppermute(mine, "core", SWAP)
    top, last = first_rows(core, mine, other, width)

    pieces, last = lax.optimization_barrier((pieces, last))
    pieces = pieces + swapped + [lax.ppermute(p, "core", SWAP) for p in pieces[1:]]
    end = last_rows(last)
    count = rows
    for axis in FINE:
        count *= lax.axis_size(axis)
    return whiten_and_score(examples, top, end, pieces, float(count) ** 0.5)


def score_kernel(scale, tile, step, x_ref, top_ref, end_ref, *refs):
    *q_refs, w_hbm, s_ref, high, low, w_ref, r_ref, sent = refs
    n = high.shape[0]
    for at, part in ((0, top_ref[...]), (n - B, end_ref[...])):
        rows = slice(at, at + part.shape[0])
        part = part * scale
        head = part.astype(jnp.bfloat16)
        high[rows, :] = head
        low[rows, :] = (part - head.astype(jnp.float32)).astype(jnp.bfloat16)
    dims = (((1,), (1,)), ((), ()))
    wide = 2 * B
    copies = []
    for t in range(0, x_ref.shape[0], tile):
        x = x_ref[t : t + tile, :]
        for at in range(0, n, wide):
            end = at + wide
            part = lax.dot_general(
                x[:, :end], high[at:end, :end], dims, preferred_element_type=jnp.float32
            ) + lax.dot_general(x[:, :end], low[at:end, :end], dims, preferred_element_type=jnp.float32)
            w_ref[t : t + tile, at:end] = part
            r_ref[t : t + tile, at:end] = part.astype(jnp.bfloat16)
        here = pl.ds(t, tile)
        copies.append(pltpu.make_async_copy(w_ref.at[here], w_hbm.at[here], sent.at[t // tile]))
        copies[-1].start()
    rounded = r_ref[...]
    best = None
    for q_ref in q_refs:
        for m in range(0, q_ref.shape[0], step):
            values = lax.dot_general(
                q_ref[m : m + step, :], rounded, dims, preferred_element_type=jnp.float32
            )
            values = jnp.max(values.reshape(step // 8, 8, values.shape[1]), axis=0)
            best = values if best is None else jnp.maximum(best, values)
    s_ref[...] = jnp.max(best, axis=0, keepdims=True)
    for copy in copies:
        copy.wait()


def whiten_and_score(x, top, end, queries, scale):
    rows, width = x.shape
    tile = 256
    whitened, scores = pl.pallas_call(
        functools.partial(score_kernel, scale, tile, 256),
        out_shape=(
            jax.ShapeDtypeStruct((rows, width), jnp.float32),
            jax.ShapeDtypeStruct((1, rows), jnp.float32),
        ),
        in_specs=[VMEM] * (3 + len(queries)),
        out_specs=(pl.BlockSpec(memory_space=pl.ANY), VMEM),
        scratch_shapes=[
            pltpu.VMEM((width, width), jnp.bfloat16),
            pltpu.VMEM((width, width), jnp.bfloat16),
            pltpu.VMEM((rows, width), jnp.float32),
            pltpu.VMEM((rows, width), jnp.bfloat16),
            pltpu.SemaphoreType.DMA((rows // tile,)),
        ],
        compiler_params=pltpu.CompilerParams(vmem_limit_bytes=24 << 20),
        name="score",
    )(x, top, end, *queries)
    return whitened, scores.reshape(rows)


def solution(mesh):
    fine = Mesh(mesh.devices.reshape(2, 4, 2, 4, 4), FINE)
    placed = (P(FINE, None), P(("y", "z_hi"), None))
    return jax.shard_map(
        body, mesh=fine, in_specs=placed, out_specs=(P(FINE, None), P(FINE)), check_vma=False
    )
```

```python
import functools
import itertools

import jax
import jax.numpy as jnp
from jax import lax
from jax.experimental import pallas as pl
from jax.experimental.pallas import tpu as pltpu
from jax.sharding import Mesh, PartitionSpec as P

FINE = ("z_lo", "x", "core", "y", "z_hi")
B = 128
SWAP = [(0, 1), (1, 0)]
W = 16
VMEM = pl.BlockSpec(memory_space=pltpu.VMEM)
SMEM = pl.BlockSpec(memory_space=pltpu.SMEM)


def exact_dot(a, b, dims):
    return lax.dot_general(
        a, b, (dims, ((), ())), precision=lax.Precision.HIGHEST, preferred_element_type=jnp.float32
    )


def gram_kernel(core_ref, x_ref, mine_ref, other_ref, packed):
    width = x_ref.shape[1]
    count = width // B
    at = 0
    for i in range(0, count, 2):
        left = x_ref[:, i * B : (i + 2) * B]
        part = lax.dot_general(
            left, x_ref[:, i * B :], (((0,), (0,)), ((), ())), preferred_element_type=jnp.float32
        )
        for r in range(2):
            for j in range(i + r, count):
                packed[at * B : (at + 1) * B, :] = part[r * B : (r + 1) * B, (j - i) * B : (j - i + 1) * B]
                at += 1
    half = mine_ref.shape[0]
    core = core_ref[0]
    mine_ref[...] = packed[pl.ds(pl.multiple_of(core * half, 8), half), :]
    other_ref[...] = packed[pl.ds(pl.multiple_of((1 - core) * half, 8), half), :]


def local_gram(core, x):
    count = x.shape[1] // B
    rows = count * (count + 1) // 2 * B
    half = jax.ShapeDtypeStruct((rows // 2, B), jnp.float32)
    return pl.pallas_call(
        gram_kernel,
        out_shape=(half, half),
        in_specs=[SMEM, VMEM],
        out_specs=(VMEM, VMEM),
        scratch_shapes=[pltpu.VMEM((rows, B), jnp.float32)],
        compiler_params=pltpu.CompilerParams(vmem_limit_bytes=16 << 20),
        name="gram",
    )(core, x)


def spread(x, lane):
    return jnp.take_along_axis(x, jnp.full(x.shape, lane, jnp.int32), axis=1)


def tree_sum(terms):
    terms = list(terms)
    while len(terms) > 1:
        pairs = [a + b for a, b in zip(terms[::2], terms[1::2])]
        terms = pairs + terms[len(pairs) * 2 :]
    return terms[0]


def gram_of_rows(s):
    high = s.astype(jnp.bfloat16)
    rest = s - high.astype(jnp.float32)
    mid = rest.astype(jnp.bfloat16)
    low = (rest - mid.astype(jnp.float32)).astype(jnp.bfloat16)
    return lax.dot_general(
        jnp.concatenate([high, high, mid, high, low, mid], 0),
        jnp.concatenate([high, mid, high, low, high, mid], 0),
        (((0,), (0,)), ((), ())),
        preferred_element_type=jnp.float32,
    )


def eliminate(a):
    n = a.shape[0]
    panels = n // W
    lane = lax.broadcasted_iota(jnp.int32, (W, n), 1)
    sub = lax.broadcasted_iota(jnp.int32, (W, n), 0)

    def row(x, j):
        return jnp.broadcast_to(x[j : j + 1], (W, n))

    out = []
    groups = [a[p * W : (p + 1) * W] for p in range(panels)]
    for p in range(panels):
        c = p * W
        here = (lane >= c) & (lane < c + W)
        cols = [spread(groups[p], c + k) for k in range(W)]
        low = jnp.where(here, jnp.where(lane - c == sub, 1.0, 0.0), groups[p])
        full = low
        inverse = jnp.ones((W, n), jnp.float32)
        for j in range(W):
            one = 1.0 / row(cols[j], j)
            ratio = jnp.where(sub == j, 0.0, cols[j] * one)
            inverse = jnp.where(sub == j, one, inverse)
            for k in range(j + 1, W):
                cols[k] = cols[k] - ratio * row(cols[k], j)
            full = full - ratio * row(full, j)
            low = low - jnp.where(sub > j, ratio, 0.0) * row(low, j)
        low = low * (lax.rsqrt(inverse) * inverse)
        out.append(jnp.where(lane < c + W, low, 0.0))
        if p < panels - 1:
            full = full * inverse
            near = tree_sum(spread(groups[p + 1], c + k) * row(full, k) for k in range(W))
            groups[p + 1] = jnp.where(here, 0.0, groups[p + 1]) - near
            if p < panels - 2:
                far = gram_of_rows(low)
                for g in range(p + 2, panels):
                    groups[g] = jnp.where(here, 0.0, groups[g]) - far[g * W : (g + 1) * W]
    return jnp.concatenate(out, 0)


def factor_step(k, count, state, top, put):
    def rows(i):
        return slice((i - top) * B, (i - top + 1) * B)

    def cols(j):
        return slice(j * B, (j + 1) * B)

    inv = eliminate(state[rows(k), cols(k)])
    right = {}
    for j in range(k + 1, count):
        right[j] = exact_dot(inv, state[rows(k), cols(j)], ((1,), (0,)))
        if j == k + 1:
            state[rows(j), cols(j)] = state[rows(j), cols(j)] - exact_dot(right[j], right[j], ((0,), (0,)))
    left = inv
    if k > 0:
        left = jnp.concatenate([exact_dot(inv, state[rows(k), : k * B], ((1,), (0,))), inv], 1)
    if k == count - 1:
        put(left)
        return
    put(jnp.concatenate([left, jnp.zeros((B, (count - 1 - k) * B), jnp.float32)], 1))
    for i in range(k + 1, count):
        for j in range(i, count):
            if j > k + 1:
                state[rows(i), cols(j)] = state[rows(i), cols(j)] - exact_dot(right[i], right[j], ((0,), (0,)))
        new = exact_dot(right[i], left, ((0,), (0,)))
        if k > 0:
            state[rows(i), : k * B] = state[rows(i), : k * B] - new[:, : k * B]
        state[rows(i), cols(k)] = -new[:, k * B :]


def first_kernel(core_ref, mine_ref, other_ref, o_ref, last_ref, packed, state):
    half = mine_ref.shape[0]
    core = core_ref[0]
    packed[pl.ds(pl.multiple_of(core * half, 8), half), :] = mine_ref[...]
    packed[pl.ds(pl.multiple_of((1 - core) * half, 8), half), :] = other_ref[...]
    count = o_ref.shape[1] // B
    at = 0
    for i in range(count):
        for j in range(i, count):
            state[i * B : (i + 1) * B, j * B : (j + 1) * B] = packed[at * B : (at + 1) * B, :]
            at += 1
    for k in range(count - 1):

        def put(value, k=k):
            o_ref[k * B : (k + 1) * B, :] = value

        factor_step(k, count, state, 0, put)
    last_ref[...] = state[(count - 1) * B :, :]


def two_parts(x):
    high = x.astype(jnp.bfloat16)
    return high, (x - high.astype(jnp.float32)).astype(jnp.bfloat16)


def times_rows(x, parts):
    high, low = (
        lax.dot_general(x, part, (((1,), (1,)), ((), ())), preferred_element_type=jnp.float32) for part in parts
    )
    return high + low


def last_kernel(scale, state_ref, x_ref, top_ref, o_ref, w_ref):
    count = o_ref.shape[1] // B
    wide = w_ref.shape[1]
    parts = two_parts(top_ref[:wide, :wide] * scale)
    for t in range(0, x_ref.shape[0], wide):
        w_ref[t : t + wide, :] = times_rows(x_ref[t : t + wide, :wide], parts)

    def put(value):
        o_ref[...] = value

    factor_step(count - 1, count, state_ref, count - 1, put)


def first_rows(core, mine, other, n):
    return pl.pallas_call(
        first_kernel,
        out_shape=(jax.ShapeDtypeStruct((n - B, n), jnp.float32), jax.ShapeDtypeStruct((B, n), jnp.float32)),
        in_specs=[SMEM, VMEM, VMEM],
        out_specs=(VMEM, VMEM),
        scratch_shapes=[pltpu.VMEM((2 * mine.shape[0], B), jnp.float32), pltpu.VMEM((n, n), jnp.float32)],
        compiler_params=pltpu.CompilerParams(vmem_limit_bytes=16 << 20),
        name="factor",
    )(core, mine, other)


def last_rows(state, x, top, scale):
    return pl.pallas_call(
        functools.partial(last_kernel, scale),
        out_shape=(
            jax.ShapeDtypeStruct(state.shape, jnp.float32),
            jax.ShapeDtypeStruct((x.shape[0], 2 * B), jnp.float32),
        ),
        in_specs=[VMEM, VMEM, VMEM],
        out_specs=(VMEM, VMEM),
        compiler_params=pltpu.CompilerParams(vmem_limit_bytes=16 << 20),
        name="factor_end",
    )(state, x, top)


def steps(move):
    shape = [lax.axis_size(axis) for axis in FINE]
    places = list(itertools.product(*map(range, shape)))
    number = {place: i for i, place in enumerate(places)}
    length = max(n for place in places for n, by in zip(shape, move(place)) if by)

    def source(place, k):
        return number[tuple((at + k * by) % n for at, by, n in zip(place, move(place), shape))]

    return [[(source(place, k), number[place]) for place in places] for k in range(1, length)]


def gather(own, move):
    return [own] + [lax.ppermute(own, FINE, step) for step in steps(move)]


def along_z():
    shape = [lax.axis_size(axis) for axis in FINE]
    places = list(itertools.product(*map(range, shape)))
    number = {place: i for i, place in enumerate(places)}

    def source(place, by):
        return number[(*place[:4], (place[4] + by) % shape[4])]

    return (
        [(source(place, -1 if place[2] else 1), number[place]) for place in places],
        [(source(place, 2), number[place]) for place in places if place[2]],
    )


def along_one(place):
    return (0, 1, 0, 0, 0) if place[2] else (0, 0, 0, 1, 0)


def along_other(place):
    return (0, 0, 0, 1, 0) if place[2] else (0, 1, 0, 0, 0)


def body(examples, queries):
    rows, width = examples.shape
    count = rows
    for axis in FINE:
        count *= lax.axis_size(axis)
    scale = float(count) ** 0.5
    plane = lax.axis_size("x") * lax.axis_size("y")
    depth = lax.axis_size("z_lo") * lax.axis_size("z_hi")
    index = lax.axis_index("core").astype(jnp.int32)
    share = queries.shape[0] // lax.axis_size("x")
    piece = lax.dynamic_slice_in_dim(queries, lax.axis_index("x") * share, share, 0)
    beside, across = (lax.ppermute(piece, FINE, step) for step in along_z())
    pieces = [jnp.where(index == 0, piece, across), beside]

    core = index.reshape(1)
    mine, other = local_gram(core, examples)
    mine = mine + lax.ppermute(other, "core", SWAP)
    part = jnp.sum(lax.all_to_all(mine.reshape(plane, -1, B), ("x", "y"), 0, 0), 0)

    pieces, part = lax.optimization_barrier((pieces, part))
    pieces = gather(jnp.concatenate(pieces, 0), along_one)

    spread = jnp.broadcast_to(part[None], (depth, *part.shape))
    part = jnp.sum(lax.all_to_all(spread, ("z_lo", "z_hi"), 0, 0), 0)

    pieces, part = lax.optimization_barrier((pieces, part))
    pieces = gather(jnp.concatenate(pieces, 0), along_other)
    swapped = [lax.ppermute(pieces[0], "core", SWAP)]

    spread = jnp.broadcast_to(part[None], (plane, *part.shape))
    mine = lax.all_to_all(spread, ("x", "y"), 0, 0).reshape(mine.shape)
    other = lax.ppermute(mine, "core", SWAP)
    top, last = first_rows(core, mine, other, width)

    pieces, last = lax.optimization_barrier((pieces, last))
    pieces = pieces + swapped + [lax.ppermute(p, "core", SWAP) for p in pieces[1:]]
    end, first = last_rows(last, examples, top, scale)
    return whiten_and_score(examples, top, end, first, pieces, scale)


def score_kernel(scale, tile, step, x_ref, top_ref, end_ref, first_ref, *refs):
    *q_refs, w_hbm, s_ref, high, low, w_ref, r_ref, sent = refs
    n = top_ref.shape[1]
    done = first_ref.shape[1]
    for at, part in ((0, top_ref[done:, :]), (n - B - done, end_ref[...])):
        rows = slice(at, at + part.shape[0])
        high[rows, :], low[rows, :] = two_parts(part * scale)
    wide = 2 * B
    copies = []
    for t in range(0, x_ref.shape[0], tile):
        x = x_ref[t : t + tile, :]
        part = first_ref[t : t + tile, :]
        w_ref[t : t + tile, :done] = part
        r_ref[t : t + tile, :done] = part.astype(jnp.bfloat16)
        for at in range(done, n, wide):
            end = at + wide
            rows = slice(at - done, end - done)
            part = times_rows(x[:, :end], (high[rows, :end], low[rows, :end]))
            w_ref[t : t + tile, at:end] = part
            r_ref[t : t + tile, at:end] = part.astype(jnp.bfloat16)
        here = pl.ds(t, tile)
        copies.append(pltpu.make_async_copy(w_ref.at[here], w_hbm.at[here], sent.at[t // tile]))
        copies[-1].start()
    rounded = r_ref[...]
    best = None
    for q_ref in q_refs:
        for m in range(0, q_ref.shape[0], step):
            values = lax.dot_general(
                q_ref[m : m + step, :], rounded, (((1,), (1,)), ((), ())), preferred_element_type=jnp.float32
            )
            values = jnp.max(values.reshape(step // 8, 8, values.shape[1]), axis=0)
            best = values if best is None else jnp.maximum(best, values)
    s_ref[...] = jnp.max(best, axis=0, keepdims=True)
    for copy in copies:
        copy.wait()


def whiten_and_score(x, top, end, first, queries, scale):
    rows, width = x.shape
    tile = 256
    rest = width - first.shape[1]
    whitened, scores = pl.pallas_call(
        functools.partial(score_kernel, scale, tile, 256),
        out_shape=(
            jax.ShapeDtypeStruct((rows, width), jnp.float32),
            jax.ShapeDtypeStruct((1, rows), jnp.float32),
        ),
        in_specs=[VMEM] * (4 + len(queries)),
        out_specs=(pl.BlockSpec(memory_space=pl.ANY), VMEM),
        scratch_shapes=[
            pltpu.VMEM((rest, width), jnp.bfloat16),
            pltpu.VMEM((rest, width), jnp.bfloat16),
            pltpu.VMEM((rows, width), jnp.float32),
            pltpu.VMEM((rows, width), jnp.bfloat16),
            pltpu.SemaphoreType.DMA((rows // tile,)),
        ],
        compiler_params=pltpu.CompilerParams(vmem_limit_bytes=20 << 20),
        name="score",
    )(x, top, end, first, *queries)
    return whitened, scores.reshape(rows)


def solution(mesh):
    fine = Mesh(mesh.devices.reshape(2, 4, 2, 4, 4), FINE)
    placed = (P(FINE, None), P(("y", "z_hi"), None))
    return jax.shard_map(
        body, mesh=fine, in_specs=placed, out_specs=(P(FINE, None), P(FINE)), check_vma=False
    )
```
